128 devices in a mesh: row: 16 (over y, z_hi, core), col: 8 (over x, z_lo).
Axes of the slice: x: 4, y: 4, z: 4 (z_hi: 2, z_lo: 2; z = z_hi * 2 + z_lo), core: 2. Of those that a mesh axis runs over, the one named last changes fastest.
Arguments:
- front: float32 [16384, 16384], P('row', 'col'), may hold values from -6 to 6
- child_upd: bfloat16 [16384, 8192], P('row', 'col'), may hold values from -6 to 6
- child_map: int32 [2, 64], replicated, may hold values from 0 to 127, as said below
- diag_inv: float32 [4, 128, 128], replicated, may hold values from -0.1875 to 0.1875
Outputs:
- factored: float32 [16384, 16384], P('row', 'col')
- panels: bfloat16 [16384, 512], P('row')
The draws below stay inside these ranges and needn't reach their ends.
Inputs may be any that keep to these rules, and one draw needn't show every extreme that they name: `child_map`: within each child the 64 entries are distinct. Each aligned group of 8 consecutive entries of one child holds every residue modulo 8 exactly once, hence distinct residues modulo 16 too.
All inputs are finite; a program needn't handle non-finite values.
Results may differ from the reference program's by a relative error of at most 0.0039.
Values may be sent and summed in bfloat16 or wider, within the bound.
A program may use at most 128 MiB of HBM per device.

```python
import jax
import jax.numpy as jnp
from jax import lax

BLOCK = 128
PANELS = 4
RB_DEV = 8
CB_DEV = 16
NB = 128
CN = 64
N_ROW = 16
N_COL = 8


def draw_child_map(key, part):
    key = jax.random.fold_in(key, 7)
    key_perm, key_half, key_shift = jax.random.split(key, 3)
    perm_keys = jax.random.split(key_perm, 2 * N_COL)
    residues = jax.vmap(lambda sub_key: jax.random.permutation(sub_key, N_COL))(perm_keys).reshape(2, N_COL, N_COL)
    upper_half = jax.random.randint(key_half, (2, N_COL, N_COL), 0, N_ROW // N_COL)
    dest_row = residues + N_COL * upper_half
    onehot = (dest_row[..., None] == jnp.arange(N_ROW)[None, None, None, :]).astype(jnp.int32)
    seen_count = jnp.sum(onehot, axis=2)
    earlier = jnp.cumsum(seen_count, axis=1) - seen_count
    occurrence = jnp.sum(onehot * earlier[:, :, None, :], axis=3)
    shift_table = jax.random.randint(key_shift, (2, N_ROW), 0, RB_DEV)
    shift_value = jnp.sum(onehot * shift_table[:, None, None, :], axis=3)
    local_block = (occurrence + shift_value) % RB_DEV
    return (local_block * N_ROW + dest_row).reshape(2, CN).astype(jnp.int32)


def level_of(stream_key, dims, cuts, low, high):
    gain, own = 1.0, jax.random.fold_in(stream_key, 6)
    for axis_at, blocks in cuts:
        heights = jnp.exp(jax.random.uniform(jax.random.fold_in(own, axis_at), (blocks,), jnp.float32, low / len(cuts), high / len(cuts)))
        gain = gain * jnp.repeat(heights, dims[axis_at] // blocks).reshape([-1 if axis == axis_at else 1 for axis in range(len(dims))])
    return gain


def bell_draw(rng, extent, spread, reach, pieces=(), kind=jnp.bfloat16):
    array = spread * jax.random.normal(rng, extent, jnp.float32)
    if pieces:
        array = array * level_of(rng, extent, pieces, -0.22, 0.18)
    return jnp.clip(array, -reach, reach).astype(kind)


def setup_inputs(seed: int = 0) -> dict:
    keys = jax.random.split(jax.random.key(seed), 5)
    return {
        "front": bell_draw(keys[0], (NB * BLOCK, NB * BLOCK), 1.0, 6.0, ((0, 16), (1, 8)), jnp.float32),
        "child_upd": bell_draw(keys[1], (2 * CN * BLOCK, CN * BLOCK), 1.0, 6.0, ((0, 16), (1, 8))),
        "child_map": draw_child_map(jax.random.fold_in(keys[4], 71), 0),
        "diag_inv": bell_draw(keys[3], (PANELS, BLOCK, BLOCK), (0.5 * BLOCK ** -0.75), 0.1875, (), jnp.float32),
    }


def row_position(global_block):
    return (global_block % N_ROW) * RB_DEV + global_block // N_ROW


def col_position(global_block):
    return (global_block % N_COL) * CB_DEV + global_block // N_COL


def reference(front, child_upd, child_map, diag_inv):
    stored = jnp.arange(NB).astype(jnp.int32)
    global_row = (stored % RB_DEV) * N_ROW + stored // RB_DEV
    global_col = (stored % CB_DEV) * N_COL + stored // CB_DEV
    assembled = front.reshape(NB, BLOCK, NB, BLOCK)
    updates = child_upd.astype(jnp.float32).reshape(2, CN, BLOCK, CN, BLOCK).transpose(0, 1, 3, 2, 4)
    row_target = row_position(child_map)[:, :, None]
    col_target = col_position(child_map)[:, None, :]
    assembled = assembled.at[row_target, :, col_target, :].add(updates)
    front_now = assembled.reshape(NB * BLOCK, NB * BLOCK)
    panel_list = []
    for panel_idx in range(PANELS):
        col_slot = (panel_idx % N_COL) * CB_DEV + panel_idx // N_COL
        column = front_now[:, col_slot * BLOCK:(col_slot + 1) * BLOCK]
        candidate = jnp.dot(column, diag_inv[panel_idx].T, precision=lax.Precision.HIGHEST, preferred_element_type=jnp.float32)
        keep_rows = jnp.repeat(global_row > panel_idx, BLOCK)
        rows_panel = jnp.where(keep_rows[:, None], candidate, jnp.zeros_like(candidate)).astype(jnp.bfloat16)
        cols_panel = rows_panel.reshape(NB, BLOCK, BLOCK)[row_position(global_col)].reshape(NB * BLOCK, BLOCK)
        front_now = front_now - jnp.dot(rows_panel, cols_panel.T, preferred_element_type=jnp.float32)
        panel_list.append(rows_panel)
    return front_now, jnp.concatenate(panel_list, axis=1)
```

```python
import jax
import jax.numpy as jnp
from jax import lax
from jax.experimental import pallas as pl
from jax.experimental.pallas import tpu as pltpu

MESH = pl.DeviceIdType.MESH
BLK = 128
HI = lax.Precision.HIGHEST
COL_STEPS = ((0, 1), (1, 0), (3, 0), (1, 1), (3, 1), (2, 0), (2, 1))
TOP_AT = (0, 0, 1, 3)


def exchange_kernel(
    cm, upd_hbm, front_hbm, dinv,
    r3, lr, lc, tab,
    upd, fcol, s1, r1, r2, wsel, rw, acol, ab, tp, tt, tf, lb, xa,
    load_sem, c_s, c_r, z_s, z_r, z_l, y_s, y_r, y_l, w_s, w_r, w_l,
    a_s, a_r, tp_s, tp_r, tb_s, tb_r, tc_s, tc_r,
    lr_s, lr_r, lr_l, al_s, al_r, be_s, be_r, be_l, fo_s, fo_r,
):
    r = lax.axis_index("row")
    c = lax.axis_index("col")
    y, zc = r // 4, lax.rem(r, 4)
    x, zl = c // 2, lax.rem(c, 2)
    child, group = r // 8, lax.rem(r, 8)

    load_upd = [
        pltpu.make_async_copy(upd_hbm.at[:, :, pl.ds(b * BLK, BLK)], upd.at[b], load_sem.at[b]) for b in range(8)
    ]
    load_col = pltpu.make_async_copy(front_hbm.at[:, pl.ds(0, BLK)], fcol, load_sem.at[8])
    for copy in load_upd:
        copy.start()
    load_col.start()

    def col_to(dx, dz):
        return lax.rem(x + dx, 4) * 2 + lax.rem(zl + dz, 2)

    def col_from(dx, dz):
        return lax.rem(x + 4 - dx, 4) * 2 + lax.rem(zl + dz, 2)

    def zc_at(d):
        return lax.rem(zc // 2 + d // 2, 2) * 2 + lax.rem(zc + d % 2, 2)

    def row_at(dy, dzc):
        return lax.rem(y + dy, 4) * 4 + zc_at(dzc)

    def send(src, dst, ssem, rsem, to):
        copy = pltpu.make_async_remote_copy(
            src_ref=src, dst_ref=dst, send_sem=ssem, recv_sem=rsem, device_id=to, device_id_type=MESH
        )
        copy.start()
        return copy

    def arrived(dst, sem):
        pltpu.make_async_copy(dst, dst, sem).wait()

    flip_r, flip_c = child * 8 + c, lax.rem(r, 8)
    off_diag = lax.rem(r, 8) != c
    barrier = pltpu.get_barrier_semaphore()
    for dx, dz in COL_STEPS:
        pl.semaphore_signal(barrier, inc=1, device_id=(r, col_to(dx, dz)), device_id_type=MESH)
    for dy in range(4):
        for d in range(4):
            if dy or d:
                pl.semaphore_signal(barrier, inc=1, device_id=(row_at(dy, d), c), device_id_type=MESH)

    @pl.when(off_diag)
    def _():
        pl.semaphore_signal(barrier, inc=1, device_id=(flip_r, flip_c), device_id_type=MESH)

    def find(first, count, modulus, residue):
        at = jnp.int32(0)
        for i in range(count):
            at = jnp.where(lax.rem(cm[child, first + i], modulus) == residue, i, at)
        return at

    block_row = [find(group * 8, 8, 8, (q % 2) * 4 + q // 2) for q in range(8)]

    for copy in load_upd:
        copy.wait()
    pl.semaphore_wait(barrier, 22 + off_diag.astype(jnp.int32))

    def pack(dst, at, to_col):
        block_col = find(c * 8, 8, 8, to_col)
        for q in range(8):
            dst[at, q] = upd[block_col, block_row[q]]

    sends = []
    for t, (dx, dz) in enumerate(COL_STEPS):
        to = col_to(dx, dz)
        pack(s1, to, to)
        sends.append(send(s1.at[to], r1.at[c], c_s.at[t], c_r.at[t], (r, to)))
    pack(r1, c, c)
    r1[8] = jnp.zeros((8, BLK, BLK), jnp.bfloat16)
    rw[16] = jnp.zeros((BLK, BLK), jnp.bfloat16)

    def col_table(at, carry):
        slot = jnp.int32(0)
        for i in range(8):
            entry = cm[at // 8, lax.rem(at, 8) * 8 + i]
            slot = jnp.where(lax.rem(entry, 8) == c, lax.div(entry, 8), slot)
        tab[16 + at] = slot
        return carry

    lax.fori_loop(0, 16, col_table, 0)

    def row_table(s):
        def step(e, found):
            entry = cm[s, e]
            return tuple(jnp.where(entry == l * 16 + r, s * 8 + e // 8, found[l]) for l in range(8))

        found = lax.fori_loop(0, 64, step, (jnp.int32(16),) * 8)
        for l in range(8):
            tab[s * 8 + l] = found[l]

    row_table(0)
    row_table(1)

    own_col = [c] + [col_from(dx, dz) for dx, dz in COL_STEPS]

    def z_stage(t):
        c0 = own_col[t]
        for d in range(1, 4):
            to = zc_at(d)
            sends.append(
                send(r1.at[c0, pl.ds(to * 2, 2)], r2.at[c0, :, zc], z_s.at[t, d - 1], z_r.at[t, d - 1], (y * 4 + to, c))
            )
        pltpu.make_async_copy(r1.at[c0, pl.ds(zc * 2, 2)], r2.at[c0, :, zc], z_l.at[t]).start()

    def y_stage(t):
        c0 = own_col[t]
        for d in range(1, 4):
            arrived(r2.at[c0, :, zc_at(d)], z_r.at[t, d - 1])
        arrived(r2.at[c0, :, zc], z_l.at[t])
        for dy in range(1, 4):
            to = lax.rem(y + dy, 4)
            sends.append(
                send(r2.at[c0, lax.rem(to, 2)], r3.at[y, c0], y_s.at[t, dy - 1], y_r.at[t, dy - 1], (to * 4 + zc, c))
            )
        pltpu.make_async_copy(r2.at[c0, lax.rem(y, 2)], r3.at[y, c0], y_l.at[t]).start()

    in_window = c < 4

    def window_send():
        source = jnp.int32(8)
        for i in range(8):
            source = jnp.where(tab[16 + child * 8 + i] == 0, i, source)
        for q in range(8):
            wsel[q] = r1[source, q]
        for dy in range(4):
            for d in range(4):
                i = dy * 4 + d
                to_y, to_zc = lax.rem(y + dy, 4), zc_at(d)
                src = wsel.at[to_zc * 2 + lax.rem(to_y, 2)]
                if i == 0:
                    pltpu.make_async_copy(src, rw.at[r], w_l).start()
                else:
                    send(src, rw.at[r], w_s.at[i], w_r.at[i], (to_y * 4 + to_zc, c))

    z_stage(0)
    for t in range(1, 8):
        arrived(r1.at[own_col[t]], c_r.at[t - 1])
        if t == 7:
            pl.when(in_window)(window_send)
        z_stage(t)
        y_stage(t - 1)
    y_stage(7)

    load_col.wait()

    @pl.when(in_window)
    def _():
        for dy in range(4):
            for d in range(4):
                i = dy * 4 + d
                src = lax.rem(y + 4 - dy, 4) * 4 + zc_at(d)
                arrived(rw.at[src], w_r.at[i] if i else w_l)
        for l in range(8):
            total = fcol[pl.ds(l * BLK, BLK), :]
            for s in range(2):
                total = total + rw[tab[s * 8 + l]].astype(jnp.float32)
            acol[l] = total
        ab[c] = acol[c]
        for l in range(8):
            @pl.when(c != l)
            def _():
                send(acol.at[l], ab.at[c], a_s.at[l], a_r.at[c], (r, l))

        @pl.when((r >= 1) & (r <= 3) & (c < r))
        def _():
            tp[c] = acol[0, pl.ds(pl.multiple_of(c * 16, 16), 16), :]
            for l in range(8):
                @pl.when(c != l)
                def _():
                    send(acol.at[0, pl.ds(l * 16, 16)], tp.at[c], tp_s.at[l], tp_r.at[c], (r, l))

    for i in (1, 2, 3):
        span = pl.ds(TOP_AT[i], i)

        @pl.when(r == i)
        def _():
            for k in range(i):
                @pl.when(c != k)
                def _():
                    arrived(tp.at[k], tp_r.at[k])
            tt[span] = tp[pl.ds(0, i)]
            for to in range(16):
                if to != i:
                    send(tp.at[pl.ds(0, i)], tt.at[span], tb_s.at[to], tb_r.at[i - 1], (to, c))

    for i in (1, 2, 3):
        span = pl.ds(TOP_AT[i], i)

        @pl.when(r != i)
        def _():
            arrived(tt.at[span], tb_r.at[i - 1])

    for t, (dx, dz) in enumerate(COL_STEPS):
        sends.append(send(tt, tf.at[c], tc_s.at[t], tc_r.at[t], (r, col_to(dx, dz))))
    tf[c] = tt[...]
    for t, (dx, dz) in enumerate(COL_STEPS):
        arrived(tf.at[col_from(dx, dz)], tc_r.at[t])
    for k in range(4):
        @pl.when(c != k)
        def _():
            arrived(ab.at[k], a_r.at[k])

    glob = c * 16 + r
    kept = []
    for k in range(4):
        parts = [ab[k]]
        for i in (1, 2, 3):
            if k < i:
                parts.append(tf[:, TOP_AT[i] + k].reshape(BLK, BLK))
        first = k + 1
        stack = jnp.concatenate(parts, axis=0) if len(parts) > 1 else parts[0]
        for j in range(k):
            rows_j, tops_j = kept[j]
            mine = [rows_j] + [tops_j[i] for i in range(first, 4)]
            mine = jnp.concatenate(mine, axis=0) if len(mine) > 1 else mine[0]
            stack = stack - lax.dot_general(
                mine, tops_j[k], (((1,), (1,)), ((), ())), preferred_element_type=jnp.float32
            )
        prod = lax.dot_general(
            stack, dinv[k], (((1,), (1,)), ((), ())), precision=HI, preferred_element_type=jnp.float32
        ).astype(jnp.bfloat16)
        own = prod[:BLK]
        own = jnp.where(glob > k, own, jnp.zeros_like(own))
        tops = {i: prod[(i - k) * BLK:(i - k + 1) * BLK] for i in range(first, 4)}
        kept.append((own, tops))
        lb[:, pl.ds(k * BLK, BLK)] = own

    @pl.when(off_diag)
    def _():
        send(lb, xa, al_s, al_r, (flip_r, flip_c))

    @pl.when(jnp.logical_not(off_diag))
    def _():
        pltpu.make_async_copy(lb, xa, al_r).start()

    for t, (dx, dz) in enumerate(COL_STEPS):
        sends.append(send(lb, lr.at[c], lr_s.at[t], lr_r.at[t], (r, col_to(dx, dz))))
    own_lr = pltpu.make_async_copy(lb, lr.at[c], lr_l)
    own_lr.start()

    arrived(xa, al_r)

    def slot(row):
        return 2 * lax.rem(row, 8) + row // 8

    spread = [(dy, d) for dy in range(4) for d in (0, 2) if dy or d]
    for i, (dy, d) in enumerate(spread):
        sends.append(send(xa, lc.at[slot(r)], be_s.at[i], be_r.at[i], (row_at(dy, d), c)))
    other = row_at(0, 1)
    sends.append(send(xa, lc.at[slot(r)], fo_s.at[7], fo_r.at[7], (other, c)))
    own_lc = pltpu.make_async_copy(xa, lc.at[slot(r)], be_l)
    own_lc.start()
    for i, (dy, d) in enumerate(spread):
        at = slot(lax.rem(y + 4 - dy, 4) * 4 + zc_at(d))
        arrived(lc.at[at], be_r.at[i])
        sends.append(send(lc.at[at], lc.at[at], fo_s.at[i], fo_r.at[i], (other, c)))

    for i, (dy, d) in enumerate(spread):
        arrived(lc.at[slot(lax.rem(y + 4 - dy, 4) * 4 + zc_at(d + 1))], fo_r.at[i])
    arrived(lc.at[slot(other)], fo_r.at[7])
    for t, (dx, dz) in enumerate(COL_STEPS):
        arrived(lr.at[col_from(dx, dz)], lr_r.at[t])
    own_lr.wait()
    own_lc.wait()
    for t in range(8):
        for dy in range(1, 4):
            arrived(r3.at[lax.rem(y + 4 - dy, 4), own_col[t]], y_r.at[t, dy - 1])
        arrived(r3.at[y, own_col[t]], y_l.at[t])
    for copy in sends:
        copy.wait_send()

    @pl.when(off_diag)
    def _():
        arrived(lb, al_s)

    @pl.when(in_window)
    def _():
        for i in range(1, 16):
            arrived(wsel.at[0], w_s.at[i])
        for l in range(8):
            @pl.when(c != l)
            def _():
                arrived(acol.at[l], a_s.at[l])

        @pl.when((r >= 1) & (r <= 3) & (c < r))
        def _():
            for l in range(8):
                @pl.when(c != l)
                def _():
                    arrived(acol.at[0, pl.ds(l * 16, 16)], tp_s.at[l])

    for i in (1, 2, 3):
        @pl.when(r == i)
        def _():
            for to in range(16):
                if to != i:
                    arrived(tp.at[pl.ds(0, i)], tb_s.at[to])


def exchange(child_map, child_upd, front, diag_inv):
    bf, f32 = jnp.bfloat16, jnp.float32
    dma = pltpu.SemaphoreType.DMA
    any_spec = pl.BlockSpec(memory_space=pl.ANY)
    smem = pl.BlockSpec(memory_space=pltpu.SMEM)
    return pl.pallas_call(
        exchange_kernel,
        out_shape=(
            jax.ShapeDtypeStruct((4, 8, 4, BLK, BLK), bf),
            jax.ShapeDtypeStruct((8, BLK, 4 * BLK), bf),
            jax.ShapeDtypeStruct((16, BLK, 4 * BLK), bf),
            jax.ShapeDtypeStruct((32,), jnp.int32),
        ),
        in_specs=[smem, any_spec, any_spec, pl.BlockSpec(memory_space=pltpu.VMEM)],
        out_specs=(any_spec, any_spec, any_spec, smem),
        scratch_shapes=[
            pltpu.VMEM((8, 8, BLK, BLK), bf),
            pltpu.VMEM((8 * BLK, BLK), f32),
            pltpu.VMEM((8, 8, BLK, BLK), bf),
            pltpu.VMEM((9, 8, BLK, BLK), bf),
            pltpu.VMEM((8, 2, 4, BLK, BLK), bf),
            pltpu.VMEM((8, BLK, BLK), bf),
            pltpu.VMEM((17, BLK, BLK), bf),
            pltpu.VMEM((8, BLK, BLK), f32),
            pltpu.VMEM((4, BLK, BLK), f32),
            pltpu.VMEM((4, 16, BLK), f32),
            pltpu.VMEM((6, 16, BLK), f32),
            pltpu.VMEM((8, 6, 16, BLK), f32),
            pltpu.VMEM((BLK, 4 * BLK), bf),
            pltpu.VMEM((BLK, 4 * BLK), bf),
            dma((9,)), dma((7,)), dma((7,)), dma((8, 3)), dma((8, 3)), dma((8,)),
            dma((8, 3)), dma((8, 3)), dma((8,)), dma((16,)), dma((16,)), dma,
            dma((8,)), dma((4,)), dma((8,)), dma((4,)), dma((16,)), dma((3,)), dma((7,)), dma((7,)),
            dma((7,)), dma((7,)), dma, dma, dma, dma((7,)), dma((7,)), dma, dma((8,)), dma((8,)),
        ],
        compiler_params=pltpu.CompilerParams(
            collective_id=0, has_side_effects=True, vmem_limit_bytes=60 * 2**20
        ),
    )(child_map, child_upd.reshape(8, BLK, 8 * BLK), front, diag_inv)


def update_kernel(tab, front, rows, cols, upd0, upd1, out, panels):
    l = pl.program_id(0)
    panels[...] = rows[0]
    out[...] = front[...] - lax.dot_general(
        rows[0], cols[...].reshape(16 * BLK, 4 * BLK), (((1,), (1,)), ((), ())),
        preferred_element_type=jnp.float32,
    )
    for s, upd in ((0, upd0), (1, upd1)):
        @pl.when(tab[s * 8 + l] < 16)
        def _():
            for c0 in range(8):
                at = pl.ds(pl.multiple_of(tab[16 + s * 8 + c0] * BLK, BLK), BLK)
                out[:, at] += upd[0, c0, 0].astype(jnp.float32)


def update(tab, front, rows, cols, arrived):
    def upd_spec(s):
        def index(l, tab):
            source = jnp.minimum(tab[s * 8 + l], 15)
            return (source // 4, 0, lax.rem(source, 4), 0, 0)

        return pl.BlockSpec((1, 8, 1, BLK, BLK), index)

    return pl.pallas_call(
        update_kernel,
        out_shape=(
            jax.ShapeDtypeStruct(front.shape, jnp.float32),
            jax.ShapeDtypeStruct((8 * BLK, 4 * BLK), jnp.bfloat16),
        ),
        grid_spec=pltpu.PrefetchScalarGridSpec(
            num_scalar_prefetch=1,
            grid=(8,),
            in_specs=[
                pl.BlockSpec((BLK, 16 * BLK), lambda l, tab: (l, 0)),
                pl.BlockSpec((1, BLK, 4 * BLK), lambda l, tab: (l, 0, 0)),
                pl.BlockSpec((16, BLK, 4 * BLK), lambda l, tab: (0, 0, 0)),
                upd_spec(0),
                upd_spec(1),
            ],
            out_specs=(
                pl.BlockSpec((BLK, 16 * BLK), lambda l, tab: (l, 0)),
                pl.BlockSpec((BLK, 4 * BLK), lambda l, tab: (l, 0)),
            ),
        ),
        compiler_params=pltpu.CompilerParams(vmem_limit_bytes=60 * 2**20),
    )(tab, front, rows, cols, arrived, arrived)


def on_device(front, child_upd, child_map, diag_inv):
    arrived, rows, cols, tab = exchange(child_map, child_upd, front, diag_inv)
    return update(tab, front, rows, cols, arrived)


def solution(mesh):
    return jax.shard_map(
        on_device,
        mesh=mesh,
        in_specs=(P("row", "col"), P("row", "col"), P(), P()),
        out_specs=(P("row", "col"), P("row", None)),
        check_vma=False,
    )


P = jax.sharding.PartitionSpec
```

```python
import jax
import jax.numpy as jnp
from jax import lax
from jax.experimental import pallas as pl
from jax.experimental.pallas import tpu as pltpu

MESH = pl.DeviceIdType.MESH
BLK = 128
HI = lax.Precision.HIGHEST
COL_STEPS = ((0, 1), (1, 0), (3, 0), (1, 1), (3, 1), (2, 0), (2, 1))
TOP_AT = (0, 0, 1, 3)


def exchange_kernel(
    cm, upd_hbm, front_hbm, dinv_hbm,
    r3, lr, lc, fvm, tab,
    upd, fcol, dinv, s1, r1, r2, wsel, rw, acol, ab, tops, tpart, tsum, tall, tp, tt, tmix, tf, bt, lb, xa, lp,
    load_sem, c_s, c_r, z_s, z_r, z_l, y_s, y_r, y_l, w_s, w_r, w_l,
    a_s, a_r, te_s, te_r, tv_s, tv_r, tp_s, tp_r, tb_s, tb_r, tc_s, tc_r,
    lp_s, lp_r, lr_s, lr_r, lr_l, al_s, al_r, be_s, be_r, be_l, fo_s, fo_r,
):
    r = lax.axis_index("row")
    c = lax.axis_index("col")
    y, zc = r // 4, lax.rem(r, 4)
    x, zl = c // 2, lax.rem(c, 2)
    child, group = r // 8, lax.rem(r, 8)

    load_upd = [
        pltpu.make_async_copy(upd_hbm.at[:, :, pl.ds(b * BLK, BLK)], upd.at[b], load_sem.at[b]) for b in range(8)
    ]
    load_col = pltpu.make_async_copy(front_hbm.at[:, pl.ds(0, BLK)], fcol, load_sem.at[8])
    for copy in load_upd:
        copy.start()
    load_col.start()
    load_dinv = pltpu.make_async_copy(dinv_hbm, dinv, load_sem.at[10])
    load_dinv.start()
    load_front = pltpu.make_async_copy(front_hbm, fvm, load_sem.at[9])

    def col_to(dx, dz):
        return lax.rem(x + dx, 4) * 2 + lax.rem(zl + dz, 2)

    def col_from(dx, dz):
        return lax.rem(x + 4 - dx, 4) * 2 + lax.rem(zl + dz, 2)

    def zc_at(d):
        return lax.rem(zc // 2 + d // 2, 2) * 2 + lax.rem(zc + d % 2, 2)

    def row_at(dy, dzc):
        return lax.rem(y + dy, 4) * 4 + zc_at(dzc)

    def send(src, dst, ssem, rsem, to):
        copy = pltpu.make_async_remote_copy(
            src_ref=src, dst_ref=dst, send_sem=ssem, recv_sem=rsem, device_id=to, device_id_type=MESH
        )
        copy.start()
        return copy

    def arrived(dst, sem):
        pltpu.make_async_copy(dst, dst, sem).wait()

    flip_r, flip_c = child * 8 + c, lax.rem(r, 8)
    flip_r2 = child * 8 + lax.rem(c // 2 + 1, 2) * 2 + c // 4 * 4 + lax.rem(c, 2)
    flip_c2 = lax.rem(flip_c // 2 + 1, 2) * 2 + flip_c // 4 * 4 + lax.rem(flip_c, 2)
    off_diag = lax.rem(r, 8) != c
    pair_at = lax.rem(c // 2, 2)
    barrier = pltpu.get_barrier_semaphore()
    for dx, dz in COL_STEPS:
        pl.semaphore_signal(barrier, inc=1, device_id=(r, col_to(dx, dz)), device_id_type=MESH)
    for dy in range(4):
        for d in range(4):
            if dy or d:
                pl.semaphore_signal(barrier, inc=1, device_id=(row_at(dy, d), c), device_id_type=MESH)

    @pl.when(off_diag)
    def _():
        pl.semaphore_signal(barrier, inc=1, device_id=(flip_r, flip_c), device_id_type=MESH)

    pl.semaphore_signal(barrier, inc=1, device_id=(flip_r, flip_c2), device_id_type=MESH)

    def residues(first):
        return [cm[child, first + i] & 7 for i in range(8)]

    def find(values, wanted):
        at = jnp.int32(0)
        for i in range(1, 8):
            at = jnp.where(values[i] == wanted, i, at)
        return at

    row_residues, col_residues = residues(group * 8), residues(c * 8)
    block_row = [find(row_residues, (q % 2) * 4 + q // 2) for q in range(8)]

    for copy in load_upd:
        copy.wait()

    def pack(dst, at, to_col):
        block_col = find(col_residues, to_col)
        for q in range(8):
            dst[at, q] = upd[block_col, block_row[q]]

    sends = []

    def c_send(t):
        to = col_to(*COL_STEPS[t])
        sends.append(send(s1.at[to], r1.at[c], c_s.at[t], c_r.at[t], (r, to)))

    def sixteen(at):
        return pl.ds(pl.multiple_of(at * 16, 16), 16)

    for dx, dz in COL_STEPS:
        to = col_to(dx, dz)
        pack(s1, to, to)
    pl.semaphore_wait(barrier, 23 + off_diag.astype(jnp.int32))
    for t in range(3):
        c_send(t)
    pack(r1, c, c)
    r1[8] = jnp.zeros((8, BLK, BLK), jnp.bfloat16)
    rw[16] = jnp.zeros((BLK, BLK), jnp.bfloat16)
    upd[8] = jnp.zeros((8, BLK, BLK), jnp.bfloat16)

    def col_table(at, carry):
        slot = jnp.int32(0)
        for i in range(8):
            entry = cm[at >> 3, (at & 7) * 8 + i]
            slot = jnp.where((entry & 7) == c, entry >> 3, slot)
        tab[16 + at] = slot
        return carry

    lax.fori_loop(0, 16, col_table, 0)

    def row_table(s):
        def step(e, found):
            entry = cm[s, e]
            here = s * 8 + (e >> 3)
            return tuple(jnp.where(entry == l * 16 + r, here, found[l]) for l in range(8))

        found = lax.fori_loop(0, 64, step, (jnp.int32(16),) * 8)
        for l in range(8):
            tab[s * 8 + l] = found[l]

    row_table(0)
    row_table(1)

    own_col = [c] + [col_from(dx, dz) for dx, dz in COL_STEPS]

    def c_wait(t):
        arrived(r1.at[own_col[t]], c_r.at[t - 1])

    def z_stage(t):
        c0 = own_col[t]
        for d in range(1, 4):
            to = zc_at(d)
            sends.append(
                send(r1.at[c0, pl.ds(to * 2, 2)], r2.at[c0, :, zc], z_s.at[t, d - 1], z_r.at[t, d - 1], (y * 4 + to, c))
            )
        pltpu.make_async_copy(r1.at[c0, pl.ds(zc * 2, 2)], r2.at[c0, :, zc], z_l.at[t]).start()

    def y_stage(t):
        c0 = own_col[t]
        for d in range(1, 4):
            arrived(r2.at[c0, :, zc_at(d)], z_r.at[t, d - 1])
        arrived(r2.at[c0, :, zc], z_l.at[t])
        for dy in range(1, 4):
            to = lax.rem(y + dy, 4)
            sends.append(
                send(r2.at[c0, lax.rem(to, 2)], r3.at[y, c0], y_s.at[t, dy - 1], y_r.at[t, dy - 1], (to * 4 + zc, c))
            )
        pltpu.make_async_copy(r2.at[c0, lax.rem(y, 2)], r3.at[y, c0], y_l.at[t]).start()

    in_window = c < 4

    def window_send():
        source = jnp.int32(8)
        for i in range(8):
            source = jnp.where(tab[16 + child * 8 + i] == 0, i, source)
        for q in range(8):
            wsel[q] = r1[source, q]
        for dy in range(4):
            for d in range(4):
                i = dy * 4 + d
                to_y, to_zc = lax.rem(y + dy, 4), zc_at(d)
                src = wsel.at[to_zc * 2 + lax.rem(to_y, 2)]
                if i == 0:
                    pltpu.make_async_copy(src, rw.at[r], w_l).start()
                else:
                    send(src, rw.at[r], w_s.at[i], w_r.at[i], (to_y * 4 + to_zc, c))

    pumped = {}

    def pump(t):
        if t - 3 in pumped:
            for copy in pumped.pop(t - 3):
                copy.wait_send()
        first = len(sends)
        y_stage(t)
        pumped[t] = sends[first:]
        del sends[first:]

    def find_equal(first, value, none):
        at = jnp.int32(none)
        for i in range(8):
            at = jnp.where(cm[child, first + i] == value, i, at)
        return at

    z_stage(0)
    top_row = [find_equal(group * 8, i, 8) for i in (1, 2, 3)]
    top_col = [find_equal(c * 8, k, 8) for k in range(3)]
    for i in (1, 2, 3):
        for k in range(i):
            at_col = jnp.where(top_row[i - 1] == 8, 8, top_col[k])
            tops[TOP_AT[i] + k] = upd[at_col, jnp.minimum(top_row[i - 1], 7)]
    for t, (dx, dz) in enumerate(COL_STEPS):
        to = col_to(dx, dz)
        sends.append(send(tops.at[:, sixteen(to)], tpart.at[c], te_s.at[t], te_r.at[t], (r, to)))
    tpart[c] = tops[:, sixteen(c), :]
    for t in range(3, 6):
        c_send(t)
    load_col.wait()
    load_dinv.wait()
    holds_top = (r >= 1) & (r <= 3) & (c < r)

    @pl.when(holds_top)
    def _():
        tp[c] = fcol[sixteen(c), :]
        for l in range(8):
            @pl.when(c != l)
            def _():
                send(fcol.at[pl.ds(l * 16, 16)], tp.at[c], tp_s.at[l], tp_r.at[c], (r, l))

    load_front.start()
    pump(0)
    for t in (1, 2, 3):
        c_wait(t)
        z_stage(t)
    c_send(6)

    for t, (dx, dz) in enumerate(COL_STEPS):
        arrived(tpart.at[col_from(dx, dz)], te_r.at[t])
    total = tpart[0].astype(jnp.float32)
    for i in range(1, 8):
        total = total + tpart[i].astype(jnp.float32)
    tsum[...] = total.astype(jnp.bfloat16)
    for dy in range(4):
        for d in range(4):
            i = dy * 4 + d
            if i:
                sends.append(send(tsum, tall.at[r], tv_s.at[i], tv_r.at[i], (row_at(dy, d), c)))
    tall[r] = tsum[...]
    for i in (1, 2, 3):
        span = pl.ds(TOP_AT[i], i)

        @pl.when(r == i)
        def _():
            for k in range(i):
                @pl.when(c != k)
                def _():
                    arrived(tp.at[k], tp_r.at[k])
            tt[span] = tp[pl.ds(0, i)]
            for to in range(16):
                if to != i:
                    send(tp.at[pl.ds(0, i)], tt.at[span], tb_s.at[to], tb_r.at[i - 1], (to, c))

    pump(1)
    for t in (4, 5, 6):
        c_wait(t)
        z_stage(t)
    pump(2)
    pump(3)

    for i in (1, 2, 3):
        span = pl.ds(TOP_AT[i], i)

        @pl.when(r != i)
        def _():
            arrived(tt.at[span], tb_r.at[i - 1])

    for dy in range(4):
        for d in range(4):
            i = dy * 4 + d
            if i:
                arrived(tall.at[lax.rem(y + 4 - dy, 4) * 4 + zc_at(d)], tv_r.at[i])
    total = tt[...]
    for i in range(16):
        total = total + tall[i].astype(jnp.float32)
    tmix[...] = total
    for t, (dx, dz) in enumerate(COL_STEPS):
        sends.append(send(tmix, tf.at[c], tc_s.at[t], tc_r.at[t], (r, col_to(dx, dz))))
    tf[c] = tmix[...]

    c_wait(7)
    pl.when(in_window)(window_send)
    z_stage(7)
    pump(4)

    for t, (dx, dz) in enumerate(COL_STEPS):
        arrived(tf.at[col_from(dx, dz)], tc_r.at[t])

    def outer(a, b):
        return lax.dot_general(a, b, (((1,), (1,)), ((), ())), preferred_element_type=jnp.float32)

    def solve(a, k):
        return lax.dot_general(
            a, dinv[k], (((1,), (1,)), ((), ())), precision=HI, preferred_element_type=jnp.float32
        ).astype(jnp.bfloat16)

    for k in range(3):
        stack = []
        for i in range(k + 1, 4):
            block = tf[:, TOP_AT[i] + k].reshape(BLK, BLK)
            for j in range(k):
                block = block - outer(bt[TOP_AT[i] + j], bt[TOP_AT[k] + j])
            stack.append(block)
        prod = solve(jnp.concatenate(stack, axis=0), k)
        for i in range(k + 1, 4):
            bt[TOP_AT[i] + k] = prod[(i - k - 1) * BLK:(i - k) * BLK]

    pump(5)

    @pl.when(in_window)
    def _():
        for dy in range(4):
            for d in range(4):
                i = dy * 4 + d
                src = lax.rem(y + 4 - dy, 4) * 4 + zc_at(d)
                arrived(rw.at[src], w_r.at[i] if i else w_l)
        for l in range(8):
            total = fcol[pl.ds(l * BLK, BLK), :]
            for s in range(2):
                total = total + rw[tab[s * 8 + l]].astype(jnp.float32)
            acol[l] = total
        ab[c] = acol[c]
        for l in range(8):
            @pl.when(c != l)
            def _():
                send(acol.at[l], ab.at[c], a_s.at[l], a_r.at[c], (r, l))

    pump(6)
    for k in range(4):
        @pl.when(c != k)
        def _():
            arrived(ab.at[k], a_r.at[k])

    glob = c * 16 + r
    kept = []
    for k in range(4):
        block = ab[k]
        for j in range(k):
            block = block - outer(kept[j], bt[TOP_AT[k] + j])
        panel = solve(block, k)
        panel = jnp.where(glob > k, panel, jnp.zeros_like(panel))
        kept.append(panel)
        lb[:, pl.ds(k * BLK, BLK)] = panel

    zh, core = zc // 2, lax.rem(zc, 2)
    sends.append(send(lb, xa.at[pair_at], al_s.at[1], al_r.at[1], (flip_r2, flip_c)))

    @pl.when(off_diag)
    def _():
        send(lb, xa.at[pair_at], al_s.at[0], al_r.at[0], (flip_r, flip_c))

    @pl.when(jnp.logical_not(off_diag))
    def _():
        pltpu.make_async_copy(lb, xa.at[pair_at], al_r.at[0]).start()

    sends.append(send(lb, lp.at[zl], lp_s, lp_r, (r, col_to(0, 1))))
    lp[zl] = lb[...]

    def x_at(dx):
        return lax.rem(x + dx, 4)

    arrived(lp.at[lax.rem(zl + 1, 2)], lp_r)
    for dx in (1, 3, 2):
        sends.append(send(lp, lr.at[x], lr_s.at[dx], lr_r.at[dx], (r, x_at(dx) * 2 + zl)))
    own_lr = pltpu.make_async_copy(lp, lr.at[x], lr_l)
    own_lr.start()

    pump(7)
    arrived(xa.at[zh], al_r.at[0])
    arrived(xa.at[lax.rem(zh + 1, 2)], al_r.at[1])
    other = row_at(0, 1)
    for dy in (1, 3, 2):
        sends.append(send(xa, lc.at[y, core], be_s.at[dy], be_r.at[dy], (row_at(dy, 0), c)))
    sends.append(send(xa, lc.at[y, core], fo_s.at[0], fo_r.at[0], (other, c)))
    own_lc = pltpu.make_async_copy(xa, lc.at[y, core], be_l)
    own_lc.start()
    for dy in (1, 3, 2):
        at = lc.at[lax.rem(y + 4 - dy, 4), core]
        arrived(at, be_r.at[dy])
        sends.append(send(at, at, fo_s.at[dy], fo_r.at[dy], (other, c)))

    load_front.wait()
    for dy in range(4):
        arrived(lc.at[lax.rem(y + 4 - dy, 4), lax.rem(core + 1, 2)], fo_r.at[dy])
    for dx in (1, 3, 2):
        arrived(lr.at[x_at(4 - dx)], lr_r.at[dx])
    own_lr.wait()
    own_lc.wait()
    for t in range(8):
        for dy in range(1, 4):
            arrived(r3.at[lax.rem(y + 4 - dy, 4), own_col[t]], y_r.at[t, dy - 1])
        arrived(r3.at[y, own_col[t]], y_l.at[t])
    for copies in [sends, *pumped.values()]:
        for copy in copies:
            copy.wait_send()

    @pl.when(off_diag)
    def _():
        arrived(lb, al_s.at[0])

    @pl.when(in_window)
    def _():
        for i in range(1, 16):
            arrived(wsel.at[0], w_s.at[i])
        for l in range(8):
            @pl.when(c != l)
            def _():
                arrived(acol.at[l], a_s.at[l])

    @pl.when(holds_top)
    def _():
        for l in range(8):
            @pl.when(c != l)
            def _():
                arrived(fcol.at[pl.ds(l * 16, 16)], tp_s.at[l])

    for i in (1, 2, 3):
        @pl.when(r == i)
        def _():
            for to in range(16):
                if to != i:
                    arrived(tp.at[pl.ds(0, i)], tb_s.at[to])


def exchange(child_map, child_upd, front, diag_inv):
    bf, f32 = jnp.bfloat16, jnp.float32
    dma = pltpu.SemaphoreType.DMA
    any_spec = pl.BlockSpec(memory_space=pl.ANY)
    smem = pl.BlockSpec(memory_space=pltpu.SMEM)
    return pl.pallas_call(
        exchange_kernel,
        out_shape=(
            pltpu.VMEM((4, 8, 4, BLK, BLK), bf),
            pltpu.VMEM((4, 2, BLK, 4 * BLK), bf),
            pltpu.VMEM((4, 2, 2, BLK, 4 * BLK), bf),
            pltpu.VMEM(front.shape, f32),
            jax.ShapeDtypeStruct((32,), jnp.int32),
        ),
        in_specs=[smem, any_spec, any_spec, any_spec],
        out_specs=(any_spec, any_spec, any_spec, any_spec, smem),
        scratch_shapes=[
            pltpu.VMEM((9, 8, BLK, BLK), bf),
            pltpu.VMEM((8 * BLK, BLK), f32),
            pltpu.VMEM((4, BLK, BLK), f32),
            pltpu.VMEM((8, 8, BLK, BLK), bf),
            pltpu.VMEM((9, 8, BLK, BLK), bf),
            pltpu.VMEM((8, 2, 4, BLK, BLK), bf),
            pltpu.VMEM((8, BLK, BLK), bf),
            pltpu.VMEM((17, BLK, BLK), bf),
            pltpu.VMEM((8, BLK, BLK), f32),
            pltpu.VMEM((4, BLK, BLK), f32),
            pltpu.VMEM((6, BLK, BLK), bf),
            pltpu.VMEM((8, 6, 16, BLK), bf),
            pltpu.VMEM((6, 16, BLK), bf),
            pltpu.VMEM((16, 6, 16, BLK), bf),
            pltpu.VMEM((4, 16, BLK), f32),
            pltpu.VMEM((6, 16, BLK), f32),
            pltpu.VMEM((6, 16, BLK), f32),
            pltpu.VMEM((8, 6, 16, BLK), f32),
            pltpu.VMEM((6, BLK, BLK), bf),
            pltpu.VMEM((BLK, 4 * BLK), bf),
            pltpu.VMEM((2, BLK, 4 * BLK), bf),
            pltpu.VMEM((2, BLK, 4 * BLK), bf),
            dma((11,)), dma((7,)), dma((7,)), dma((8, 3)), dma((8, 3)), dma((8,)),
            dma((8, 3)), dma((8, 3)), dma((8,)), dma((16,)), dma((16,)), dma,
            dma((8,)), dma((4,)), dma((7,)), dma((7,)), dma((16,)), dma((16,)),
            dma((8,)), dma((4,)), dma((16,)), dma((3,)), dma((7,)), dma((7,)),
            dma, dma, dma((4,)), dma((4,)), dma, dma((2,)), dma((2,)), dma((4,)), dma((4,)), dma, dma((4,)), dma((4,)),
        ],
        compiler_params=pltpu.CompilerParams(
            collective_id=0, has_side_effects=True, vmem_limit_bytes=48 * 2**20
        ),
    )(child_map, child_upd.reshape(8, BLK, 8 * BLK), front, diag_inv)


def update_kernel(tab, front, rows, cols, arrived, out, panels, stage, out_sem, panel_sem):
    copy_panels = pltpu.make_async_copy(rows, panels, panel_sem)
    copy_panels.start()
    mine = rows[...].reshape(8 * BLK, 4 * BLK)
    copies = []
    for t in range(8):
        at = pl.ds(t * 2 * BLK, 2 * BLK)
        pair = jnp.concatenate([cols[t // 4, t % 2, t // 2 % 2], cols[2 + t // 4, t % 2, t // 2 % 2]], axis=0)
        if t >= 2:
            copies[t - 2].wait()
        stage[t % 2] = front[:, at] - lax.dot_general(
            mine, pair, (((1,), (1,)), ((), ())), preferred_element_type=jnp.float32
        )
        for s in range(2):
            for j in range(2):
                c0 = source_col(tab, s, 2 * t + j)

                @pl.when(c0 >= 0)
                def _():
                    @pl.loop(0, 8)
                    def _(l):
                        source = tab[s * 8 + l]

                        @pl.when(source < 16)
                        def _():
                            here = (t % 2, pl.ds(pl.multiple_of(l * BLK, BLK), BLK), pl.ds(j * BLK, BLK))
                            stage[here] += arrived[source // 4, c0, lax.rem(source, 4)].astype(jnp.float32)
        copy = pltpu.make_async_copy(stage.at[t % 2], out.at[:, at], out_sem.at[t % 2])
        copy.start()
        copies.append(copy)
    copies[6].wait()
    copies[7].wait()
    copy_panels.wait()


def source_col(tab, s, slot):
    at = jnp.int32(-1)
    for i in range(8):
        at = jnp.where(tab[16 + s * 8 + i] == slot, i, at)
    return at


def update(tab, front, rows, cols, arrived):
    vmem = pl.BlockSpec(memory_space=pltpu.VMEM)
    any_spec = pl.BlockSpec(memory_space=pl.ANY)
    out, panels = pl.pallas_call(
        update_kernel,
        out_shape=(
            jax.ShapeDtypeStruct(front.shape, jnp.float32),
            jax.ShapeDtypeStruct((8, BLK, 4 * BLK), jnp.bfloat16),
        ),
        in_specs=[pl.BlockSpec(memory_space=pltpu.SMEM), vmem, vmem, vmem, vmem],
        out_specs=(any_spec, any_spec),
        scratch_shapes=[
            pltpu.VMEM((2, 8 * BLK, 2 * BLK), jnp.float32),
            pltpu.SemaphoreType.DMA((2,)),
            pltpu.SemaphoreType.DMA,
        ],
        compiler_params=pltpu.CompilerParams(vmem_limit_bytes=24 * 2**20),
    )(tab, front, rows.reshape(8, BLK, 4 * BLK), cols, arrived)
    return out, panels.reshape(8 * BLK, 4 * BLK)


def on_device(front, child_upd, child_map, diag_inv):
    arrived, rows, cols, front_near, tab = exchange(child_map, child_upd, front, diag_inv)
    return update(tab, front_near, rows, cols, arrived)


def solution(mesh):
    return jax.shard_map(
        on_device,
        mesh=mesh,
        in_specs=(P("row", "col"), P("row", "col"), P(), P()),
        out_specs=(P("row", "col"), P("row", None)),
        check_vma=False,
    )


P = jax.sharding.PartitionSpec
```

```python
import jax
import jax.numpy as jnp
from jax import lax
from jax.experimental import pallas as pl
from jax.experimental.pallas import tpu as pltpu

MESH = pl.DeviceIdType.MESH
BLK = 128
HI = lax.Precision.HIGHEST
COL_STEPS = ((0, 1), (1, 0), (3, 0), (1, 1), (3, 1), (2, 0), (2, 1))
TOP_AT = (0, 0, 1, 3)


def exchange_kernel(
    cm, upd_hbm, front_hbm, dinv_hbm,
    r3, lr, lc, fvm, tab,
    upd, fcol, dinv, s1, r1, r2, wsel, rw, acol, ab, tops, tpart, tsum, tall, tp, tt, tmix, tf, bt, lb, xa, lp,
    load_sem, c_s, c_r, z_s, z_r, z_l, y_s, y_r, y_l, w_s, w_r, w_l,
    a_s, a_r, te_s, te_r, tv_s, tv_r, tp_s, tp_r, tb_s, tb_r, tc_s, tc_r,
    lp_s, lp_r, lr_s, lr_r, lr_l, al_s, al_r, be_s, be_r, be_l, fo_s, fo_r,
):
    r = lax.axis_index("row")
    c = lax.axis_index("col")
    y, zc = r // 4, lax.rem(r, 4)
    x, zl = c // 2, lax.rem(c, 2)
    child, group = r // 8, lax.rem(r, 8)

    load_upd = [
        pltpu.make_async_copy(upd_hbm.at[:, :, pl.ds(b * BLK, BLK)], upd.at[b], load_sem.at[b]) for b in range(8)
    ]
    load_col = pltpu.make_async_copy(front_hbm.at[:, pl.ds(0, BLK)], fcol, load_sem.at[8])
    for copy in load_upd:
        copy.start()
    load_col.start()
    load_dinv = pltpu.make_async_copy(dinv_hbm, dinv, load_sem.at[10])
    load_dinv.start()
    load_front = pltpu.make_async_copy(front_hbm, fvm, load_sem.at[9])

    def col_to(dx, dz):
        return lax.rem(x + dx, 4) * 2 + lax.rem(zl + dz, 2)

    def col_from(dx, dz):
        return lax.rem(x + 4 - dx, 4) * 2 + lax.rem(zl + dz, 2)

    def zc_at(d):
        return lax.rem(zc // 2 + d // 2, 2) * 2 + lax.rem(zc + d % 2, 2)

    def row_at(dy, dzc):
        return lax.rem(y + dy, 4) * 4 + zc_at(dzc)

    def send(src, dst, ssem, rsem, to):
        copy = pltpu.make_async_remote_copy(
            src_ref=src, dst_ref=dst, send_sem=ssem, recv_sem=rsem, device_id=to, device_id_type=MESH
        )
        copy.start()
        return copy

    def arrived(dst, sem):
        pltpu.make_async_copy(dst, dst, sem).wait()

    flip_r, flip_c = child * 8 + c, lax.rem(r, 8)
    off_diag = lax.rem(r, 8) != c
    pair_at = lax.rem(c // 2, 2)
    barrier = pltpu.get_barrier_semaphore()
    for dx, dz in COL_STEPS:
        pl.semaphore_signal(barrier, inc=1, device_id=(r, col_to(dx, dz)), device_id_type=MESH)
    for dy in range(4):
        for d in range(4):
            if dy or d:
                pl.semaphore_signal(barrier, inc=1, device_id=(row_at(dy, d), c), device_id_type=MESH)

    @pl.when(off_diag)
    def _():
        pl.semaphore_signal(barrier, inc=1, device_id=(flip_r, flip_c), device_id_type=MESH)

    def residues(first):
        return [cm[child, first + i] & 7 for i in range(8)]

    def find(values, wanted):
        at = jnp.int32(0)
        for i in range(1, 8):
            at = jnp.where(values[i] == wanted, i, at)
        return at

    row_residues, col_residues = residues(group * 8), residues(c * 8)
    block_row = [find(row_residues, (q % 2) * 4 + q // 2) for q in range(8)]

    for copy in load_upd:
        copy.wait()

    def pack(dst, at, to_col):
        block_col = find(col_residues, to_col)
        for q in range(8):
            dst[at, q] = upd[block_col, block_row[q]]

    sends = []

    def c_send(t):
        to = col_to(*COL_STEPS[t])
        sends.append(send(s1.at[to], r1.at[c], c_s.at[t], c_r.at[t], (r, to)))

    def sixteen(at):
        return pl.ds(pl.multiple_of(at * 16, 16), 16)

    for dx, dz in COL_STEPS:
        to = col_to(dx, dz)
        pack(s1, to, to)
    pl.semaphore_wait(barrier, 22 + off_diag.astype(jnp.int32))
    for t in range(3):
        c_send(t)
    pack(r1, c, c)
    r1[8] = jnp.zeros((8, BLK, BLK), jnp.bfloat16)
    rw[16] = jnp.zeros((BLK, BLK), jnp.bfloat16)
    upd[8] = jnp.zeros((8, BLK, BLK), jnp.bfloat16)

    def col_table(at, carry):
        slot = jnp.int32(0)
        for i in range(8):
            entry = cm[at >> 3, (at & 7) * 8 + i]
            slot = jnp.where((entry & 7) == c, entry >> 3, slot)
        tab[16 + at] = slot
        return carry

    lax.fori_loop(0, 16, col_table, 0)

    def row_table(s):
        def step(e, found):
            entry = cm[s, e]
            here = s * 8 + (e >> 3)
            return tuple(jnp.where(entry == l * 16 + r, here, found[l]) for l in range(8))

        found = lax.fori_loop(0, 64, step, (jnp.int32(16),) * 8)
        for l in range(8):
            tab[s * 8 + l] = found[l]

    row_table(0)
    row_table(1)

    own_col = [c] + [col_from(dx, dz) for dx, dz in COL_STEPS]

    def c_wait(t):
        arrived(r1.at[own_col[t]], c_r.at[t - 1])

    def z_stage(t):
        c0 = own_col[t]
        for d in range(1, 4):
            to = zc_at(d)
            sends.append(
                send(r1.at[c0, pl.ds(to * 2, 2)], r2.at[c0, :, zc], z_s.at[t, d - 1], z_r.at[t, d - 1], (y * 4 + to, c))
            )
        pltpu.make_async_copy(r1.at[c0, pl.ds(zc * 2, 2)], r2.at[c0, :, zc], z_l.at[t]).start()

    def y_stage(t):
        c0 = own_col[t]
        for d in range(1, 4):
            arrived(r2.at[c0, :, zc_at(d)], z_r.at[t, d - 1])
        arrived(r2.at[c0, :, zc], z_l.at[t])
        for dy in range(1, 4):
            to = lax.rem(y + dy, 4)
            sends.append(
                send(r2.at[c0, lax.rem(to, 2)], r3.at[y, c0], y_s.at[t, dy - 1], y_r.at[t, dy - 1], (to * 4 + zc, c))
            )
        pltpu.make_async_copy(r2.at[c0, lax.rem(y, 2)], r3.at[y, c0], y_l.at[t]).start()

    in_window = c < 4

    def window_send():
        source = jnp.int32(8)
        for i in range(8):
            source = jnp.where(tab[16 + child * 8 + i] == 0, i, source)
        for q in range(8):
            wsel[q] = r1[source, q]
        for dy in range(4):
            for d in range(4):
                i = dy * 4 + d
                to_y, to_zc = lax.rem(y + dy, 4), zc_at(d)
                src = wsel.at[to_zc * 2 + lax.rem(to_y, 2)]
                if i == 0:
                    pltpu.make_async_copy(src, rw.at[r], w_l).start()
                else:
                    send(src, rw.at[r], w_s.at[i], w_r.at[i], (to_y * 4 + to_zc, c))

    pumped = {}

    def pump(t):
        if t - 3 in pumped:
            for copy in pumped.pop(t - 3):
                copy.wait_send()
        first = len(sends)
        y_stage(t)
        pumped[t] = sends[first:]
        del sends[first:]

    def find_equal(first, value, none):
        at = jnp.int32(none)
        for i in range(8):
            at = jnp.where(cm[child, first + i] == value, i, at)
        return at

    z_stage(0)
    top_row = [find_equal(group * 8, i, 8) for i in (1, 2, 3)]
    top_col = [find_equal(c * 8, k, 8) for k in range(3)]
    for i in (1, 2, 3):
        for k in range(i):
            at_col = jnp.where(top_row[i - 1] == 8, 8, top_col[k])
            tops[TOP_AT[i] + k] = upd[at_col, jnp.minimum(top_row[i - 1], 7)]
    for t, (dx, dz) in enumerate(COL_STEPS):
        to = col_to(dx, dz)
        sends.append(send(tops.at[:, sixteen(to)], tpart.at[c], te_s.at[t], te_r.at[t], (r, to)))
    tpart[c] = tops[:, sixteen(c), :]
    for t in range(3, 6):
        c_send(t)
    load_col.wait()
    load_dinv.wait()
    holds_top = (r >= 1) & (r <= 3) & (c < r)

    @pl.when(holds_top)
    def _():
        tp[c] = fcol[sixteen(c), :]
        for l in range(8):
            @pl.when(c != l)
            def _():
                send(fcol.at[pl.ds(l * 16, 16)], tp.at[c], tp_s.at[l], tp_r.at[c], (r, l))

    load_front.start()
    pump(0)
    for t in (1, 2, 3):
        c_wait(t)
        z_stage(t)
    c_send(6)

    for t, (dx, dz) in enumerate(COL_STEPS):
        arrived(tpart.at[col_from(dx, dz)], te_r.at[t])
    total = tpart[0].astype(jnp.float32)
    for i in range(1, 8):
        total = total + tpart[i].astype(jnp.float32)
    tsum[...] = total.astype(jnp.bfloat16)
    for dy in range(4):
        for d in range(4):
            i = dy * 4 + d
            if i:
                sends.append(send(tsum, tall.at[r], tv_s.at[i], tv_r.at[i], (row_at(dy, d), c)))
    tall[r] = tsum[...]
    for i in (1, 2, 3):
        span = pl.ds(TOP_AT[i], i)

        @pl.when(r == i)
        def _():
            for k in range(i):
                @pl.when(c != k)
                def _():
                    arrived(tp.at[k], tp_r.at[k])
            tt[span] = tp[pl.ds(0, i)]
            for to in range(16):
                if to != i:
                    send(tp.at[pl.ds(0, i)], tt.at[span], tb_s.at[to], tb_r.at[i - 1], (to, c))

    pump(1)
    for t in (4, 5, 6):
        c_wait(t)
        z_stage(t)
    pump(2)
    pump(3)

    for i in (1, 2, 3):
        span = pl.ds(TOP_AT[i], i)

        @pl.when(r != i)
        def _():
            arrived(tt.at[span], tb_r.at[i - 1])

    for dy in range(4):
        for d in range(4):
            i = dy * 4 + d
            if i:
                arrived(tall.at[lax.rem(y + 4 - dy, 4) * 4 + zc_at(d)], tv_r.at[i])
    total = tt[...]
    for i in range(16):
        total = total + tall[i].astype(jnp.float32)
    tmix[...] = total
    for t, (dx, dz) in enumerate(COL_STEPS):
        sends.append(send(tmix, tf.at[c], tc_s.at[t], tc_r.at[t], (r, col_to(dx, dz))))
    tf[c] = tmix[...]

    c_wait(7)
    pl.when(in_window)(window_send)
    z_stage(7)
    pump(4)

    for t, (dx, dz) in enumerate(COL_STEPS):
        arrived(tf.at[col_from(dx, dz)], tc_r.at[t])

    def outer(a, b):
        return lax.dot_general(a, b, (((1,), (1,)), ((), ())), preferred_element_type=jnp.float32)

    def solve(a, k):
        return lax.dot_general(
            a, dinv[k], (((1,), (1,)), ((), ())), precision=HI, preferred_element_type=jnp.float32
        ).astype(jnp.bfloat16)

    for k in range(3):
        stack = []
        for i in range(k + 1, 4):
            block = tf[:, TOP_AT[i] + k].reshape(BLK, BLK)
            for j in range(k):
                block = block - outer(bt[TOP_AT[i] + j], bt[TOP_AT[k] + j])
            stack.append(block)
        prod = solve(jnp.concatenate(stack, axis=0), k)
        for i in range(k + 1, 4):
            bt[TOP_AT[i] + k] = prod[(i - k - 1) * BLK:(i - k) * BLK]

    pump(5)

    @pl.when(in_window)
    def _():
        for dy in range(4):
            for d in range(4):
                i = dy * 4 + d
                src = lax.rem(y + 4 - dy, 4) * 4 + zc_at(d)
                arrived(rw.at[src], w_r.at[i] if i else w_l)
        for l in range(8):
            total = fcol[pl.ds(l * BLK, BLK), :]
            for s in range(2):
                total = total + rw[tab[s * 8 + l]].astype(jnp.float32)
            acol[l] = total
        ab[c] = acol[c]
        for l in range(8):
            @pl.when(c != l)
            def _():
                send(acol.at[l], ab.at[c], a_s.at[l], a_r.at[c], (r, l))

    pump(6)
    for k in range(4):
        @pl.when(c != k)
        def _():
            arrived(ab.at[k], a_r.at[k])

    glob = c * 16 + r
    kept = []
    for k in range(4):
        block = ab[k]
        for j in range(k):
            block = block - outer(kept[j], bt[TOP_AT[k] + j])
        panel = solve(block, k)
        panel = jnp.where(glob > k, panel, jnp.zeros_like(panel))
        kept.append(panel)
        lb[:, pl.ds(k * BLK, BLK)] = panel

    zh, core = zc // 2, lax.rem(zc, 2)

    @pl.when(off_diag)
    def _():
        send(lb, xa.at[pair_at], al_s.at[0], al_r.at[0], (flip_r, flip_c))

    @pl.when(jnp.logical_not(off_diag))
    def _():
        pltpu.make_async_copy(lb, xa.at[pair_at], al_r.at[0]).start()

    sends.append(send(lb, lp.at[zl], lp_s, lp_r, (r, col_to(0, 1))))
    lp[zl] = lb[...]

    def x_at(dx):
        return lax.rem(x + dx, 4)

    arrived(lp.at[lax.rem(zl + 1, 2)], lp_r)
    for dx in (1, 3, 2):
        sends.append(send(lp, lr.at[x], lr_s.at[dx], lr_r.at[dx], (r, x_at(dx) * 2 + zl)))
    own_lr = pltpu.make_async_copy(lp, lr.at[x], lr_l)
    own_lr.start()

    pump(7)
    other = row_at(0, 1)

    def spread(at, i):
        for dy in (1, 3, 2):
            sends.append(send(xa.at[at], lc.at[y, core, at], be_s.at[i, dy], be_r.at[i, dy], (row_at(dy, 0), c)))
        sends.append(send(xa.at[at], lc.at[y, core, at], fo_s.at[i, 0], fo_r.at[i, 0], (other, c)))

    def forward(at, i):
        for dy in (1, 3, 2):
            here = lc.at[lax.rem(y + 4 - dy, 4), core, at]
            arrived(here, be_r.at[i, dy])
            sends.append(send(here, here, fo_s.at[i, dy], fo_r.at[i, dy], (other, c)))

    far = 1 - zh
    arrived(xa.at[zh], al_r.at[0])
    sends.append(send(xa.at[zh], xa.at[zh], al_s.at[1], al_r.at[1], (row_at(0, 2), c)))
    spread(zh, 0)
    arrived(xa.at[far], al_r.at[1])
    spread(far, 1)
    own_lc = pltpu.make_async_copy(xa, lc.at[y, core], be_l)
    own_lc.start()
    forward(zh, 0)
    forward(far, 1)

    load_front.wait()
    for i, at in ((0, zh), (1, far)):
        for dy in range(4):
            arrived(lc.at[lax.rem(y + 4 - dy, 4), 1 - core, at], fo_r.at[i, dy])
    for dx in (1, 3, 2):
        arrived(lr.at[x_at(4 - dx)], lr_r.at[dx])
    own_lr.wait()
    own_lc.wait()
    for t in range(8):
        for dy in range(1, 4):
            arrived(r3.at[lax.rem(y + 4 - dy, 4), own_col[t]], y_r.at[t, dy - 1])
        arrived(r3.at[y, own_col[t]], y_l.at[t])
    for copies in [sends, *pumped.values()]:
        for copy in copies:
            copy.wait_send()

    @pl.when(off_diag)
    def _():
        arrived(lb, al_s.at[0])

    @pl.when(in_window)
    def _():
        for i in range(1, 16):
            arrived(wsel.at[0], w_s.at[i])
        for l in range(8):
            @pl.when(c != l)
            def _():
                arrived(acol.at[l], a_s.at[l])

    @pl.when(holds_top)
    def _():
        for l in range(8):
            @pl.when(c != l)
            def _():
                arrived(fcol.at[pl.ds(l * 16, 16)], tp_s.at[l])

    for i in (1, 2, 3):
        @pl.when(r == i)
        def _():
            for to in range(16):
                if to != i:
                    arrived(tp.at[pl.ds(0, i)], tb_s.at[to])


def exchange(child_map, child_upd, front, diag_inv):
    bf, f32 = jnp.bfloat16, jnp.float32
    dma = pltpu.SemaphoreType.DMA
    any_spec = pl.BlockSpec(memory_space=pl.ANY)
    smem = pl.BlockSpec(memory_space=pltpu.SMEM)
    return pl.pallas_call(
        exchange_kernel,
        out_shape=(
            pltpu.VMEM((4, 8, 4, BLK, BLK), bf),
            pltpu.VMEM((4, 2, BLK, 4 * BLK), bf),
            pltpu.VMEM((4, 2, 2, BLK, 4 * BLK), bf),
            pltpu.VMEM(front.shape, f32),
            jax.ShapeDtypeStruct((32,), jnp.int32),
        ),
        in_specs=[smem, any_spec, any_spec, any_spec],
        out_specs=(any_spec, any_spec, any_spec, any_spec, smem),
        scratch_shapes=[
            pltpu.VMEM((9, 8, BLK, BLK), bf),
            pltpu.VMEM((8 * BLK, BLK), f32),
            pltpu.VMEM((4, BLK, BLK), f32),
            pltpu.VMEM((8, 8, BLK, BLK), bf),
            pltpu.VMEM((9, 8, BLK, BLK), bf),
            pltpu.VMEM((8, 2, 4, BLK, BLK), bf),
            pltpu.VMEM((8, BLK, BLK), bf),
            pltpu.VMEM((17, BLK, BLK), bf),
            pltpu.VMEM((8, BLK, BLK), f32),
            pltpu.VMEM((4, BLK, BLK), f32),
            pltpu.VMEM((6, BLK, BLK), bf),
            pltpu.VMEM((8, 6, 16, BLK), bf),
            pltpu.VMEM((6, 16, BLK), bf),
            pltpu.VMEM((16, 6, 16, BLK), bf),
            pltpu.VMEM((4, 16, BLK), f32),
            pltpu.VMEM((6, 16, BLK), f32),
            pltpu.VMEM((6, 16, BLK), f32),
            pltpu.VMEM((8, 6, 16, BLK), f32),
            pltpu.VMEM((6, BLK, BLK), bf),
            pltpu.VMEM((BLK, 4 * BLK), bf),
            pltpu.VMEM((2, BLK, 4 * BLK), bf),
            pltpu.VMEM((2, BLK, 4 * BLK), bf),
            dma((11,)), dma((7,)), dma((7,)), dma((8, 3)), dma((8, 3)), dma((8,)),
            dma((8, 3)), dma((8, 3)), dma((8,)), dma((16,)), dma((16,)), dma,
            dma((8,)), dma((4,)), dma((7,)), dma((7,)), dma((16,)), dma((16,)),
            dma((8,)), dma((4,)), dma((16,)), dma((3,)), dma((7,)), dma((7,)),
            dma, dma, dma((4,)), dma((4,)), dma, dma((2,)), dma((2,)), dma((2, 4)), dma((2, 4)), dma, dma((2, 4)), dma((2, 4)),
        ],
        compiler_params=pltpu.CompilerParams(
            collective_id=0, has_side_effects=True, vmem_limit_bytes=48 * 2**20
        ),
    )(child_map, child_upd.reshape(8, BLK, 8 * BLK), front, diag_inv)


def update_kernel(tab, front, rows, cols, arrived, out, panels, stage, out_sem, panel_sem):
    copy_panels = pltpu.make_async_copy(rows, panels, panel_sem)
    copy_panels.start()
    copies = []
    for t in range(8):
        at = pl.ds(t * 2 * BLK, 2 * BLK)
        pair = jnp.concatenate([cols[t // 4, t % 2, t // 2 % 2], cols[2 + t // 4, t % 2, t // 2 % 2]], axis=0)
        if t >= 2:
            copies[t - 2].wait()
        for part in range(2):
            here = pl.ds(part * 4 * BLK, 4 * BLK)
            mine = rows[pl.ds(part * 4, 4)].reshape(4 * BLK, 4 * BLK)
            stage[t % 2, here, :] = front[here, at] - lax.dot_general(
                mine, pair, (((1,), (1,)), ((), ())), preferred_element_type=jnp.float32
            )
        for s in range(2):
            for j in range(2):
                c0 = source_col(tab, s, 2 * t + j)

                @pl.when(c0 >= 0)
                def _():
                    for l in range(8):
                        source = tab[s * 8 + l]

                        @pl.when(source < 16)
                        def _():
                            here = (t % 2, pl.ds(l * BLK, BLK), pl.ds(j * BLK, BLK))
                            stage[here] += arrived[source // 4, c0, lax.rem(source, 4)].astype(jnp.float32)
        copy = pltpu.make_async_copy(stage.at[t % 2], out.at[:, at], out_sem.at[t % 2])
        copy.start()
        copies.append(copy)
    copies[6].wait()
    copies[7].wait()
    copy_panels.wait()


def source_col(tab, s, slot):
    at = jnp.int32(-1)
    for i in range(8):
        at = jnp.where(tab[16 + s * 8 + i] == slot, i, at)
    return at


def update(tab, front, rows, cols, arrived):
    vmem = pl.BlockSpec(memory_space=pltpu.VMEM)
    any_spec = pl.BlockSpec(memory_space=pl.ANY)
    out, panels = pl.pallas_call(
        update_kernel,
        out_shape=(
            jax.ShapeDtypeStruct(front.shape, jnp.float32),
            jax.ShapeDtypeStruct((8, BLK, 4 * BLK), jnp.bfloat16),
        ),
        in_specs=[pl.BlockSpec(memory_space=pltpu.SMEM), vmem, vmem, vmem, vmem],
        out_specs=(any_spec, any_spec),
        scratch_shapes=[
            pltpu.VMEM((2, 8 * BLK, 2 * BLK), jnp.float32),
            pltpu.SemaphoreType.DMA((2,)),
            pltpu.SemaphoreType.DMA,
        ],
        compiler_params=pltpu.CompilerParams(vmem_limit_bytes=24 * 2**20),
    )(tab, front, rows.reshape(8, BLK, 4 * BLK), cols, arrived)
    return out, panels.reshape(8 * BLK, 4 * BLK)


def on_device(front, child_upd, child_map, diag_inv):
    arrived, rows, cols, front_near, tab = exchange(child_map, child_upd, front, diag_inv)
    return update(tab, front_near, rows, cols, arrived)


def solution(mesh):
    return jax.shard_map(
        on_device,
        mesh=mesh,
        in_specs=(P("row", "col"), P("row", "col"), P(), P()),
        out_specs=(P("row", "col"), P("row", None)),
        check_vma=False,
    )


P = jax.sharding.PartitionSpec
```

```python
import jax
import jax.numpy as jnp
from jax import lax
from jax.experimental import pallas as pl
from jax.experimental.pallas import tpu as pltpu

MESH = pl.DeviceIdType.MESH
BLK = 128
HI = lax.Precision.HIGHEST
COL_STEPS = ((0, 1), (1, 0), (3, 0), (1, 1), (3, 1), (2, 0), (2, 1))
TOP_AT = (0, 0, 1, 3)


def exchange_kernel(
    cm, upd_hbm, front_hbm, dinv_hbm,
    r3, lr, lc, fvm, tab,
    upd, fcol, dinv, s1, r1, r2, wsel, rw, acol, ab, tops, tpart, tsum, tall, tp, tt, tmix, tf, bt, lb, xa, lp,
    load_sem, c_s, c_r, z_s, z_r, z_l, y_s, y_r, y_l, w_s, w_r, w_l,
    a_s, a_r, te_s, te_r, tv_s, tv_r, tp_s, tp_r, tb_s, tb_r, tc_s, tc_r,
    lp_s, lp_r, lr_s, lr_r, lr_l, al_s, al_r, be_s, be_r, be_l, fo_s, fo_r,
):
    r = lax.axis_index("row")
    c = lax.axis_index("col")
    y, zc = r // 4, lax.rem(r, 4)
    x, zl = c // 2, lax.rem(c, 2)
    child, group = r // 8, lax.rem(r, 8)

    load_upd = [
        pltpu.make_async_copy(upd_hbm.at[:, :, pl.ds(b * BLK, BLK)], upd.at[b], load_sem.at[b]) for b in range(8)
    ]
    load_col = pltpu.make_async_copy(front_hbm.at[:, pl.ds(0, BLK)], fcol, load_sem.at[8])
    for copy in load_upd:
        copy.start()
    load_col.start()
    load_dinv = pltpu.make_async_copy(dinv_hbm, dinv, load_sem.at[10])
    load_dinv.start()
    load_front = pltpu.make_async_copy(front_hbm, fvm, load_sem.at[9])

    def col_to(dx, dz):
        return lax.rem(x + dx, 4) * 2 + lax.rem(zl + dz, 2)

    def col_from(dx, dz):
        return lax.rem(x + 4 - dx, 4) * 2 + lax.rem(zl + dz, 2)

    def zc_at(d):
        return lax.rem(zc // 2 + d // 2, 2) * 2 + lax.rem(zc + d % 2, 2)

    def row_at(dy, dzc):
        return lax.rem(y + dy, 4) * 4 + zc_at(dzc)

    def send(src, dst, ssem, rsem, to):
        copy = pltpu.make_async_remote_copy(
            src_ref=src, dst_ref=dst, send_sem=ssem, recv_sem=rsem, device_id=to, device_id_type=MESH
        )
        copy.start()
        return copy

    def arrived(dst, sem):
        pltpu.make_async_copy(dst, dst, sem).wait()

    flip_r, flip_c = child * 8 + c, lax.rem(r, 8)
    off_diag = lax.rem(r, 8) != c
    pair_at = lax.rem(c // 2, 2)
    barrier = pltpu.get_barrier_semaphore()
    for dx, dz in COL_STEPS:
        pl.semaphore_signal(barrier, inc=1, device_id=(r, col_to(dx, dz)), device_id_type=MESH)
    for dy in range(4):
        for d in range(4):
            if dy or d:
                pl.semaphore_signal(barrier, inc=1, device_id=(row_at(dy, d), c), device_id_type=MESH)

    @pl.when(off_diag)
    def _():
        pl.semaphore_signal(barrier, inc=1, device_id=(flip_r, flip_c), device_id_type=MESH)

    def residues(first):
        return [cm[child, first + i] & 7 for i in range(8)]

    def find(values, wanted):
        at = jnp.int32(0)
        for i in range(1, 8):
            at = jnp.where(values[i] == wanted, i, at)
        return at

    row_residues, col_residues = residues(group * 8), residues(c * 8)
    block_row = [find(row_residues, (q % 2) * 4 + q // 2) for q in range(8)]

    for copy in load_upd:
        copy.wait()

    def pack(dst, at, to_col):
        block_col = find(col_residues, to_col)
        for q in range(8):
            dst[at, q] = upd[block_col, block_row[q]]

    sends = []

    def c_send(t):
        to = col_to(*COL_STEPS[t])
        sends.append(send(s1.at[to], r1.at[c], c_s.at[t], c_r.at[t], (r, to)))

    def sixteen(at):
        return pl.ds(pl.multiple_of(at * 16, 16), 16)

    for dx, dz in COL_STEPS:
        to = col_to(dx, dz)
        pack(s1, to, to)
    pl.semaphore_wait(barrier, 22 + off_diag.astype(jnp.int32))
    for t in range(3):
        c_send(t)
    pack(r1, c, c)
    r1[8] = jnp.zeros((8, BLK, BLK), jnp.bfloat16)
    rw[16] = jnp.zeros((BLK, BLK), jnp.bfloat16)
    upd[8] = jnp.zeros((8, BLK, BLK), jnp.bfloat16)

    def col_table(at, carry):
        slot = jnp.int32(0)
        for i in range(8):
            entry = cm[at >> 3, (at & 7) * 8 + i]
            slot = jnp.where((entry & 7) == c, entry >> 3, slot)
        tab[16 + at] = slot
        return carry

    lax.fori_loop(0, 16, col_table, 0)

    def row_table(s):
        def step(e, found):
            entry = cm[s, e]
            here = s * 8 + (e >> 3)
            return tuple(jnp.where(entry == l * 16 + r, here, found[l]) for l in range(8))

        found = lax.fori_loop(0, 64, step, (jnp.int32(16),) * 8)
        for l in range(8):
            tab[s * 8 + l] = found[l]

    row_table(0)
    row_table(1)

    own_col = [c] + [col_from(dx, dz) for dx, dz in COL_STEPS]

    def c_wait(t):
        arrived(r1.at[own_col[t]], c_r.at[t - 1])

    def z_stage(t):
        c0 = own_col[t]
        for d in range(1, 4):
            to = zc_at(d)
            sends.append(
                send(r1.at[c0, pl.ds(to * 2, 2)], r2.at[c0, :, zc], z_s.at[t, d - 1], z_r.at[t, d - 1], (y * 4 + to, c))
            )
        pltpu.make_async_copy(r1.at[c0, pl.ds(zc * 2, 2)], r2.at[c0, :, zc], z_l.at[t]).start()

    def y_stage(t):
        c0 = own_col[t]
        for d in range(1, 4):
            arrived(r2.at[c0, :, zc_at(d)], z_r.at[t, d - 1])
        arrived(r2.at[c0, :, zc], z_l.at[t])
        for dy in range(1, 4):
            to = lax.rem(y + dy, 4)
            sends.append(
                send(r2.at[c0, lax.rem(to, 2)], r3.at[y, c0], y_s.at[t, dy - 1], y_r.at[t, dy - 1], (to * 4 + zc, c))
            )
        pltpu.make_async_copy(r2.at[c0, lax.rem(y, 2)], r3.at[y, c0], y_l.at[t]).start()

    in_window = c < 4

    def window_send():
        source = jnp.int32(8)
        for i in range(8):
            source = jnp.where(tab[16 + child * 8 + i] == 0, i, source)
        for q in range(8):
            wsel[q] = r1[source, q]
        for dy in range(4):
            for d in range(4):
                i = dy * 4 + d
                to_y, to_zc = lax.rem(y + dy, 4), zc_at(d)
                src = wsel.at[to_zc * 2 + lax.rem(to_y, 2)]
                if i == 0:
                    pltpu.make_async_copy(src, rw.at[r], w_l).start()
                else:
                    send(src, rw.at[r], w_s.at[i], w_r.at[i], (to_y * 4 + to_zc, c))

    pumped = {}

    def pump(t):
        if t - 3 in pumped:
            for copy in pumped.pop(t - 3):
                copy.wait_send()
        first = len(sends)
        y_stage(t)
        pumped[t] = sends[first:]
        del sends[first:]

    def find_equal(first, value, none):
        at = jnp.int32(none)
        for i in range(8):
            at = jnp.where(cm[child, first + i] == value, i, at)
        return at

    z_stage(0)
    top_row = [find_equal(group * 8, i, 8) for i in (1, 2, 3)]
    top_col = [find_equal(c * 8, k, 8) for k in range(3)]
    for i in (1, 2, 3):
        for k in range(i):
            at_col = jnp.where(top_row[i - 1] == 8, 8, top_col[k])
            tops[TOP_AT[i] + k] = upd[at_col, jnp.minimum(top_row[i - 1], 7)]
    for t, (dx, dz) in enumerate(COL_STEPS):
        to = col_to(dx, dz)
        sends.append(send(tops.at[:, sixteen(to)], tpart.at[c], te_s.at[t], te_r.at[t], (r, to)))
    tpart[c] = tops[:, sixteen(c), :]
    for t in range(3, 6):
        c_send(t)
    load_col.wait()
    load_dinv.wait()
    holds_top = (r >= 1) & (r <= 3) & (c < r)

    @pl.when(holds_top)
    def _():
        tp[c] = fcol[sixteen(c), :]
        for l in range(8):
            @pl.when(c != l)
            def _():
                send(fcol.at[pl.ds(l * 16, 16)], tp.at[c], tp_s.at[l], tp_r.at[c], (r, l))

    load_front.start()
    pump(0)
    for t in (1, 2, 3):
        c_wait(t)
        z_stage(t)
    c_send(6)

    for t, (dx, dz) in enumerate(COL_STEPS):
        arrived(tpart.at[col_from(dx, dz)], te_r.at[t])
    total = tpart[0].astype(jnp.float32)
    for i in range(1, 8):
        total = total + tpart[i].astype(jnp.float32)
    tsum[...] = total.astype(jnp.bfloat16)
    for dy in range(4):
        for d in range(4):
            i = dy * 4 + d
            if i:
                sends.append(send(tsum, tall.at[r], tv_s.at[i], tv_r.at[i], (row_at(dy, d), c)))
    tall[r] = tsum[...]
    for i in (1, 2, 3):
        span = pl.ds(TOP_AT[i], i)

        @pl.when(r == i)
        def _():
            for k in range(i):
                @pl.when(c != k)
                def _():
                    arrived(tp.at[k], tp_r.at[k])
            tt[span] = tp[pl.ds(0, i)]
            for to in range(16):
                if to != i:
                    send(tp.at[pl.ds(0, i)], tt.at[span], tb_s.at[to], tb_r.at[i - 1], (to, c))

    pump(1)
    for t in (4, 5, 6):
        c_wait(t)
        z_stage(t)
    pump(2)
    pump(3)

    for i in (1, 2, 3):
        span = pl.ds(TOP_AT[i], i)

        @pl.when(r != i)
        def _():
            arrived(tt.at[span], tb_r.at[i - 1])

    for dy in range(4):
        for d in range(4):
            i = dy * 4 + d
            if i:
                arrived(tall.at[lax.rem(y + 4 - dy, 4) * 4 + zc_at(d)], tv_r.at[i])
    total = tt[...]
    for i in range(16):
        total = total + tall[i].astype(jnp.float32)
    tmix[...] = total
    for t, (dx, dz) in enumerate(COL_STEPS):
        sends.append(send(tmix, tf.at[c], tc_s.at[t], tc_r.at[t], (r, col_to(dx, dz))))
    tf[c] = tmix[...]

    c_wait(7)
    pl.when(in_window)(window_send)
    z_stage(7)
    pump(4)

    for t, (dx, dz) in enumerate(COL_STEPS):
        arrived(tf.at[col_from(dx, dz)], tc_r.at[t])

    def outer(a, b):
        return lax.dot_general(a, b, (((1,), (1,)), ((), ())), preferred_element_type=jnp.float32)

    def solve(a, k):
        return lax.dot_general(
            a, dinv[k], (((1,), (1,)), ((), ())), precision=HI, preferred_element_type=jnp.float32
        ).astype(jnp.bfloat16)

    for k in range(3):
        stack = []
        for i in range(k + 1, 4):
            block = tf[:, TOP_AT[i] + k].reshape(BLK, BLK)
            for j in range(k):
                block = block - outer(bt[TOP_AT[i] + j], bt[TOP_AT[k] + j])
            stack.append(block)
        prod = solve(jnp.concatenate(stack, axis=0), k)
        for i in range(k + 1, 4):
            bt[TOP_AT[i] + k] = prod[(i - k - 1) * BLK:(i - k) * BLK]

    pump(5)

    @pl.when(in_window)
    def _():
        for dy in range(4):
            for d in range(4):
                i = dy * 4 + d
                src = lax.rem(y + 4 - dy, 4) * 4 + zc_at(d)
                arrived(rw.at[src], w_r.at[i] if i else w_l)
        for l in range(8):
            total = fcol[pl.ds(l * BLK, BLK), :]
            for s in range(2):
                total = total + rw[tab[s * 8 + l]].astype(jnp.float32)
            acol[l] = total
        ab[c] = acol[c]
        for l in range(8):
            @pl.when(c != l)
            def _():
                send(acol.at[l], ab.at[c], a_s.at[l], a_r.at[c], (r, l))

    pump(6)
    for k in range(4):
        @pl.when(c != k)
        def _():
            arrived(ab.at[k], a_r.at[k])

    glob = c * 16 + r
    kept = []
    for k in range(4):
        block = ab[k]
        for j in range(k):
            block = block - outer(kept[j], bt[TOP_AT[k] + j])
        panel = solve(block, k)
        panel = jnp.where(glob > k, panel, jnp.zeros_like(panel))
        kept.append(panel)
        lb[:, pl.ds(k * BLK, BLK)] = panel

    zh, core = zc // 2, lax.rem(zc, 2)

    @pl.when(off_diag)
    def _():
        send(lb, xa.at[pair_at], al_s.at[0], al_r.at[0], (flip_r, flip_c))

    @pl.when(jnp.logical_not(off_diag))
    def _():
        pltpu.make_async_copy(lb, xa.at[pair_at], al_r.at[0]).start()

    sends.append(send(lb, lp.at[zl], lp_s, lp_r, (r, col_to(0, 1))))
    lp[zl] = lb[...]

    def x_at(dx):
        return lax.rem(x + dx, 4)

    arrived(lp.at[lax.rem(zl + 1, 2)], lp_r)
    for dx in (1, 3, 2):
        sends.append(send(lp, lr.at[x], lr_s.at[dx], lr_r.at[dx], (r, x_at(dx) * 2 + zl)))
    own_lr = pltpu.make_async_copy(lp, lr.at[x], lr_l)
    own_lr.start()

    pump(7)
    other = row_at(0, 1)

    def spread(at, i):
        for dy in (1, 3, 2):
            sends.append(send(xa.at[at], lc.at[y, core, at], be_s.at[i, dy], be_r.at[i, dy], (row_at(dy, 0), c)))
        sends.append(send(xa.at[at], lc.at[y, core, at], fo_s.at[i, 0], fo_r.at[i, 0], (other, c)))

    def forward(at, i):
        for dy in (1, 3, 2):
            here = lc.at[lax.rem(y + 4 - dy, 4), core, at]
            arrived(here, be_r.at[i, dy])
            sends.append(send(here, here, fo_s.at[i, dy], fo_r.at[i, dy], (other, c)))

    far = 1 - zh
    arrived(xa.at[zh], al_r.at[0])
    sends.append(send(xa.at[zh], xa.at[zh], al_s.at[1], al_r.at[1], (row_at(0, 2), c)))
    spread(zh, 0)
    arrived(xa.at[far], al_r.at[1])
    spread(far, 1)
    own_lc = pltpu.make_async_copy(xa, lc.at[y, core], be_l)
    own_lc.start()
    forward(zh, 0)
    forward(far, 1)

    load_front.wait()
    for i, at in ((0, zh), (1, far)):
        for dy in range(4):
            arrived(lc.at[lax.rem(y + 4 - dy, 4), 1 - core, at], fo_r.at[i, dy])
    for dx in (1, 3, 2):
        arrived(lr.at[x_at(4 - dx)], lr_r.at[dx])
    own_lr.wait()
    own_lc.wait()
    for t in range(8):
        for dy in range(1, 4):
            arrived(r3.at[lax.rem(y + 4 - dy, 4), own_col[t]], y_r.at[t, dy - 1])
        arrived(r3.at[y, own_col[t]], y_l.at[t])
    for copies in [sends, *pumped.values()]:
        for copy in copies:
            copy.wait_send()

    @pl.when(off_diag)
    def _():
        arrived(lb, al_s.at[0])

    @pl.when(in_window)
    def _():
        for i in range(1, 16):
            arrived(wsel.at[0], w_s.at[i])
        for l in range(8):
            @pl.when(c != l)
            def _():
                arrived(acol.at[l], a_s.at[l])

    @pl.when(holds_top)
    def _():
        for l in range(8):
            @pl.when(c != l)
            def _():
                arrived(fcol.at[pl.ds(l * 16, 16)], tp_s.at[l])

    for i in (1, 2, 3):
        @pl.when(r == i)
        def _():
            for to in range(16):
                if to != i:
                    arrived(tp.at[pl.ds(0, i)], tb_s.at[to])


def exchange(child_map, child_upd, front, diag_inv):
    bf, f32 = jnp.bfloat16, jnp.float32
    dma = pltpu.SemaphoreType.DMA
    any_spec = pl.BlockSpec(memory_space=pl.ANY)
    smem = pl.BlockSpec(memory_space=pltpu.SMEM)
    return pl.pallas_call(
        exchange_kernel,
        out_shape=(
            pltpu.VMEM((4, 8, 4, BLK, BLK), bf),
            pltpu.VMEM((4, 2, BLK, 4 * BLK), bf),
            pltpu.VMEM((4, 2, 2, BLK, 4 * BLK), bf),
            pltpu.VMEM(front.shape, f32),
            pltpu.SMEM((32,), jnp.int32),
        ),
        in_specs=[smem, any_spec, any_spec, any_spec],
        out_specs=(any_spec, any_spec, any_spec, any_spec, smem),
        scratch_shapes=[
            pltpu.VMEM((9, 8, BLK, BLK), bf),
            pltpu.VMEM((8 * BLK, BLK), f32),
            pltpu.VMEM((4, BLK, BLK), f32),
            pltpu.VMEM((8, 8, BLK, BLK), bf),
            pltpu.VMEM((9, 8, BLK, BLK), bf),
            pltpu.VMEM((8, 2, 4, BLK, BLK), bf),
            pltpu.VMEM((8, BLK, BLK), bf),
            pltpu.VMEM((17, BLK, BLK), bf),
            pltpu.VMEM((8, BLK, BLK), f32),
            pltpu.VMEM((4, BLK, BLK), f32),
            pltpu.VMEM((6, BLK, BLK), bf),
            pltpu.VMEM((8, 6, 16, BLK), bf),
            pltpu.VMEM((6, 16, BLK), bf),
            pltpu.VMEM((16, 6, 16, BLK), bf),
            pltpu.VMEM((4, 16, BLK), f32),
            pltpu.VMEM((6, 16, BLK), f32),
            pltpu.VMEM((6, 16, BLK), f32),
            pltpu.VMEM((8, 6, 16, BLK), f32),
            pltpu.VMEM((6, BLK, BLK), bf),
            pltpu.VMEM((BLK, 4 * BLK), bf),
            pltpu.VMEM((2, BLK, 4 * BLK), bf),
            pltpu.VMEM((2, BLK, 4 * BLK), bf),
            dma((11,)), dma((7,)), dma((7,)), dma((8, 3)), dma((8, 3)), dma((8,)),
            dma((8, 3)), dma((8, 3)), dma((8,)), dma((16,)), dma((16,)), dma,
            dma((8,)), dma((4,)), dma((7,)), dma((7,)), dma((16,)), dma((16,)),
            dma((8,)), dma((4,)), dma((16,)), dma((3,)), dma((7,)), dma((7,)),
            dma, dma, dma((4,)), dma((4,)), dma, dma((2,)), dma((2,)), dma((2, 4)), dma((2, 4)), dma, dma((2, 4)), dma((2, 4)),
        ],
        compiler_params=pltpu.CompilerParams(
            collective_id=0, has_side_effects=True, vmem_limit_bytes=48 * 2**20
        ),
    )(child_map, child_upd.reshape(8, BLK, 8 * BLK), front, diag_inv)


def update_kernel(tab, front, rows, cols, arrived, out, panels, stage, out_sem, panel_sem):
    copy_panels = pltpu.make_async_copy(rows, panels, panel_sem)
    copy_panels.start()
    copies = []
    for t in range(8):
        at = pl.ds(t * 2 * BLK, 2 * BLK)
        pair = jnp.concatenate([cols[t // 4, t % 2, t // 2 % 2], cols[2 + t // 4, t % 2, t // 2 % 2]], axis=0)
        if t >= 2:
            copies[t - 2].wait()
        for part in range(2):
            here = pl.ds(part * 4 * BLK, 4 * BLK)
            mine = rows[pl.ds(part * 4, 4)].reshape(4 * BLK, 4 * BLK)
            stage[t % 2, here, :] = front[here, at] - lax.dot_general(
                mine, pair, (((1,), (1,)), ((), ())), preferred_element_type=jnp.float32
            )
        for s in range(2):
            for j in range(2):
                c0 = source_col(tab, s, 2 * t + j)

                @pl.when(c0 >= 0)
                def _():
                    for l in range(8):
                        source = tab[s * 8 + l]

                        @pl.when(source < 16)
                        def _():
                            here = (t % 2, pl.ds(l * BLK, BLK), pl.ds(j * BLK, BLK))
                            stage[here] += arrived[source // 4, c0, lax.rem(source, 4)].astype(jnp.float32)
        copy = pltpu.make_async_copy(stage.at[t % 2], out.at[:, at], out_sem.at[t % 2])
        copy.start()
        copies.append(copy)
    copies[6].wait()
    copies[7].wait()
    copy_panels.wait()


def source_col(tab, s, slot):
    at = jnp.int32(-1)
    for i in range(8):
        at = jnp.where(tab[16 + s * 8 + i] == slot, i, at)
    return at


def update(tab, front, rows, cols, arrived):
    vmem = pl.BlockSpec(memory_space=pltpu.VMEM)
    any_spec = pl.BlockSpec(memory_space=pl.ANY)
    out, panels = pl.pallas_call(
        update_kernel,
        out_shape=(
            jax.ShapeDtypeStruct(front.shape, jnp.float32),
            jax.ShapeDtypeStruct((8, BLK, 4 * BLK), jnp.bfloat16),
        ),
        in_specs=[pl.BlockSpec(memory_space=pltpu.SMEM), vmem, vmem, vmem, vmem],
        out_specs=(any_spec, any_spec),
        scratch_shapes=[
            pltpu.VMEM((2, 8 * BLK, 2 * BLK), jnp.float32),
            pltpu.SemaphoreType.DMA((2,)),
            pltpu.SemaphoreType.DMA,
        ],
        compiler_params=pltpu.CompilerParams(vmem_limit_bytes=24 * 2**20),
    )(tab, front, rows.reshape(8, BLK, 4 * BLK), cols, arrived)
    return out, panels.reshape(8 * BLK, 4 * BLK)


def on_device(front, child_upd, child_map, diag_inv):
    arrived, rows, cols, front_near, tab = exchange(child_map, child_upd, front, diag_inv)
    return update(tab, front_near, rows, cols, arrived)


def solution(mesh):
    return jax.shard_map(
        on_device,
        mesh=mesh,
        in_specs=(P("row", "col"), P("row", "col"), P(), P()),
        out_specs=(P("row", "col"), P("row", None)),
        check_vma=False,
    )


P = jax.sharding.PartitionSpec
```
